32 devices in a mesh: rep: 4 (over y, core), shard: 8 (over z, x).
Axes of the slice: x: 2, y: 2, z: 4, core: 2. Of those that a mesh axis runs over, the one named last changes fastest.
Arguments:
- hidden_in: bfloat16 [32768, 768], P(('rep', 'shard')), may hold values from -6 to 6
- seq_lengths: int32 [32, 8], P(('rep', 'shard')), may hold values from 0 to 1024, as said below
- norm1_scale: bfloat16 [768], P('shard'), may hold values from 0.099609375 to 1.8984375
- qkv_weight: bfloat16 [768, 2304], P('shard'), may hold values from -0.21875 to 0.21875
- out_weight: bfloat16 [768, 768], P('shard'), may hold values from -1.75 to 1.75
- norm2_scale: bfloat16 [768], P('shard'), may hold values from 0.099609375 to 1.8984375
- in_weight: bfloat16 [768, 2304], P('shard'), may hold values from -0.21875 to 0.21875
- mlp_out_weight: bfloat16 [1152, 768], P('shard'), may hold values from -0.1875 to 0.1875
- cotangent: bfloat16 [32768, 768], P(('rep', 'shard')), may hold values from -6 to 6
Outputs:
- output: bfloat16 [32768, 768], P(('rep', 'shard'))
- input_grad: bfloat16 [32768, 768], P(('rep', 'shard'))
- norm1_grad: float32 [768], P('shard')
- qkv_grad: float32 [768, 2304], P('shard')
- out_grad: float32 [768, 768], P('shard')
- norm2_grad: float32 [768], P('shard')
- in_grad: float32 [768, 2304], P('shard')
- mlp_out_grad: float32 [1152, 768], P('shard')
The draws below stay inside these ranges and needn't reach their ends.
Inputs may be any that keep to these rules, and one draw needn't show every extreme that they name: `seq_lengths`: each row lists one device's sequence lengths in order, then zeros; a nonzero length is at least 64; a row sums to at most 1024 and at least 512; some row holds a single sequence of 1024 tokens.
All inputs are finite; a program needn't handle non-finite values.
Results may differ from the reference program's by a relative error of at most 0.015.
Values may be sent and summed in bfloat16 or wider, within the bound.
A program may use at most 256 MiB of HBM per device.

```python
import jax
import jax.numpy as jnp
from jax import lax

D = 768
HEADS = 12
FF = 1152
HEAD_DIM = 64
TOK_DEV = 1024
SEQ_SLOTS = 8
MINLEN = 64
TOKENS = 32768
DEVICES = 32


def draw_seq_lengths(key, part):
    key = jax.random.fold_in(key, 7)
    key_list = jax.random.split(key, 4)
    slot_ids = jnp.arange(SEQ_SLOTS, dtype=jnp.int32)
    seq_count = jax.random.randint(key_list[0], (DEVICES, 1), 1, SEQ_SLOTS + 1)
    row_total = jax.random.randint(key_list[1], (DEVICES, 1), TOK_DEV // 2, TOK_DEV + 1)
    spare_rows = row_total - seq_count * MINLEN
    upper = jnp.broadcast_to(spare_rows + 1, (DEVICES, SEQ_SLOTS - 1))
    cut_points = jax.random.randint(key_list[2], (DEVICES, SEQ_SLOTS - 1), 0, upper)
    cut_points = jnp.where(slot_ids[None, 1:] < seq_count, cut_points, spare_rows)
    cut_points = jnp.sort(cut_points, axis=1)
    bounds = jnp.concatenate([jnp.zeros((DEVICES, 1), jnp.int32), cut_points, spare_rows], axis=1)
    pieces = bounds[:, 1:] - bounds[:, :-1]
    lengths = jnp.where(slot_ids[None, :] < seq_count, pieces + MINLEN, 0)
    full_device = jax.random.randint(key_list[3], (), 0, DEVICES)
    lone_row = jnp.where(slot_ids == 0, TOK_DEV, 0)
    chosen = jnp.arange(DEVICES, dtype=jnp.int32) == full_device
    return jnp.where(chosen[:, None], lone_row[None, :], lengths).astype(jnp.int32)


def shard_levels(key, extent, cuts, least, largest):
    gain, own = 1.0, jax.random.fold_in(key, 6)
    for dim, blocks in cuts:
        steps = jnp.exp(jax.random.uniform(jax.random.fold_in(own, dim), (blocks,), jnp.float32, least / len(cuts), largest / len(cuts)))
        gain = gain * jnp.repeat(steps, extent[dim] // blocks).reshape([-1 if axis == dim else 1 for axis in range(len(extent))])
    return gain


def gaussian(rng, dims, scale, limit, cuts=(), kind=jnp.bfloat16):
    gain = shard_levels(rng, dims, cuts, -0.22, 0.18) if cuts else 1.0
    values = jax.random.normal(rng, dims, jnp.float32) * scale * gain
    return jnp.minimum(jnp.maximum(values, -limit), limit).astype(kind)


def setup_inputs(seed: int = 0) -> dict:
    streams_of = jax.random.split(jax.random.key(seed), 10)
    return {
        "hidden_in": gaussian(streams_of[0], (TOKENS, D), 1.0, 6.0, ((0, 32),)),
        "seq_lengths": draw_seq_lengths(jax.random.fold_in(streams_of[9], 71), 0),
        "norm1_scale": jnp.clip(1.0 + 0.18 * jax.random.normal(streams_of[2], (D,), jnp.float32), 0.099609375, 1.8984375).astype(jnp.bfloat16),
        "qkv_weight": gaussian(streams_of[3], (D, 3 * D), D ** -0.5, 0.21875, ((0, 8),)),
        "out_weight": gaussian(streams_of[4], (D, D), (D // 64) ** -0.5, 1.75, ((0, 8),)),
        "norm2_scale": jnp.clip(1.0 + 0.18 * jax.random.normal(streams_of[5], (D,), jnp.float32), 0.099609375, 1.8984375).astype(jnp.bfloat16),
        "in_weight": gaussian(streams_of[6], (D, 2 * FF), D ** -0.5, 0.21875, ((0, 8),)),
        "mlp_out_weight": gaussian(streams_of[7], (FF, D), FF ** -0.5, 0.1875, ((0, 8),)),
        "cotangent": gaussian(streams_of[8], (TOKENS, D), 1.0, 6.0, ((0, 32),)),
    }


@jax.custom_vjp
def low(v):
    return lax.optimization_barrier(v.astype(jnp.bfloat16)).astype(jnp.float32)

@jax.custom_vjp
def low_back(v):
    return v

def low_keep(v):
    return (low(v), None)

def low_pass(kept, grad):
    return (grad,)

def back_keep(v):
    return (v, None)

def back_low(kept, grad):
    return (low(grad),)
low.defvjp(low_keep, low_pass)
low_back.defvjp(back_keep, back_low)
rope_base = 160000.0
norm_eps = 1e-05
masked_score = -1000000000.0

def layer_norm(values, gain_vec):
    centered = values - lax.optimization_barrier(jnp.mean(values, axis=-1, keepdims=True))
    spread = lax.optimization_barrier(jnp.mean(centered * centered, axis=-1, keepdims=True))
    return centered * lax.rsqrt(spread + norm_eps) * gain_vec

def rotary_tables(lengths, token_rows, head_width):
    seq_ends = jnp.cumsum(lengths).astype(jnp.int32)
    row_ids = jnp.arange(token_rows, dtype=jnp.int32)
    passed = row_ids[:, None] >= seq_ends[None, :]
    segment = lax.optimization_barrier(jnp.sum(passed.astype(jnp.int32), axis=1))
    starts = lax.optimization_barrier(jnp.sum(jnp.where(passed, lengths[None, :], 0), axis=1)).astype(jnp.int32)
    position = (row_ids - starts).astype(jnp.float32)
    half_width = head_width // 2
    frequency = rope_base ** (-(jnp.arange(half_width, dtype=jnp.float32) * 2.0 / head_width))
    angles = position[:, None] * frequency[None, :]
    valid_rows = (row_ids < seq_ends[-1]).astype(jnp.float32)
    return (jnp.cos(angles), jnp.sin(angles), segment, valid_rows)

def rope(tensor, cosine, sine_table):
    half_width = tensor.shape[-1] // 2
    first = tensor[..., :half_width]
    second = tensor[..., half_width:]
    cos_b = cosine[:, None, :]
    sin_b = sine_table[:, None, :]
    return jnp.concatenate([first * cos_b - second * sin_b, second * cos_b + first * sin_b], axis=-1)

def geglu(gate_up):
    hidden_units = gate_up.shape[-1] // 2
    return jax.nn.gelu(gate_up[:, :hidden_units], approximate=False) * gate_up[:, hidden_units:]

def reference(hidden_in, seq_lengths, norm1_scale, qkv_weight, out_weight, norm2_scale, in_weight, mlp_out_weight, cotangent):
    highest = lax.Precision.HIGHEST
    params = tuple((item.astype(jnp.float32) for item in (norm1_scale, qkv_weight, out_weight, norm2_scale, in_weight, mlp_out_weight)))
    inputs_all = hidden_in.astype(jnp.float32).reshape(DEVICES, TOK_DEV, D)
    cots_all = cotangent.astype(jnp.float32).reshape(DEVICES, TOK_DEV, D)
    score_scale = HEAD_DIM ** (-0.5)

    def one_device(totals_acc, pieces):
        inputs_dev, lengths, cot_dev = pieces
        cosine, sine_table, segment, valid_rows = rotary_tables(lengths, TOK_DEV, HEAD_DIM)
        same_seq = segment[:, None] == segment[None, :]

        def forward(inputs_f32, gain_one, w_qkv, w_out, gain_two, w_in, w_mlp):
            normed_one = low(layer_norm(inputs_f32, gain_one))
            projected = low_back(jnp.dot(normed_one, w_qkv, precision=highest)).reshape(TOK_DEV, 3, HEADS, HEAD_DIM)
            queries = low(rope(projected[:, 0], cosine, sine_table))
            keys_rot = low(rope(projected[:, 1], cosine, sine_table))
            values_low = low(projected[:, 2])
            scores = low_back(jnp.einsum('qhd,khd->hqk', queries, keys_rot, precision=highest) * score_scale)
            scores = jnp.where(same_seq[None], scores, masked_score)
            row_max = lax.optimization_barrier(jnp.max(scores, axis=-1, keepdims=True))
            expo = jnp.exp(scores - row_max)
            probs = low(expo / lax.optimization_barrier(jnp.sum(expo, axis=-1, keepdims=True)))
            attended = low(low_back(jnp.einsum('hqk,khd->qhd', probs, values_low, precision=highest))).reshape(TOK_DEV, D)
            resid_one = inputs_f32 + low_back(jnp.dot(attended, w_out, precision=highest))
            normed_two = low(layer_norm(resid_one, gain_two))
            gate_up = low_back(jnp.dot(normed_two, w_in, precision=highest))
            mixed = low(geglu(gate_up))
            return valid_rows[:, None] * (resid_one + low_back(jnp.dot(mixed, w_mlp, precision=highest)))
        result, back_fn = jax.vjp(forward, inputs_dev, *params)
        grads = back_fn(cot_dev)
        totals_acc = tuple((acc + grad for acc, grad in zip(totals_acc, grads[1:])))
        return (totals_acc, (result, grads[0]))
    zeros = tuple((jnp.zeros_like(item) for item in params))
    totals, (results, input_grads) = lax.scan(one_device, zeros, (inputs_all, seq_lengths, cots_all))
    return (results.reshape(TOKENS, D).astype(jnp.bfloat16), input_grads.reshape(TOKENS, D).astype(jnp.bfloat16), totals[0], totals[1], totals[2], totals[3], totals[4], totals[5])
```

```python
import functools

import jax
import jax.numpy as jnp
from jax import lax
from jax.experimental import pallas as pl
from jax.experimental.pallas import tpu as pltpu
from jax.sharding import PartitionSpec as P

HEADS = 12


rope_base = 160000.0
norm_eps = 1e-05
masked_score = -1000000000.0
log2e = 1.4426950408889634
MIB = 1024 * 1024


def layer_norm(values, gain_vec):
    centered = values - jnp.mean(values, axis=-1, keepdims=True)
    spread = jnp.mean(centered * centered, axis=-1, keepdims=True)
    return centered * lax.rsqrt(spread + norm_eps) * gain_vec


def rotary_tables(lengths, token_rows, head_width):
    seq_ends = jnp.cumsum(lengths)
    row_ids = jnp.arange(token_rows, dtype=jnp.int32)
    passed = row_ids[:, None] >= seq_ends[None, :]
    segment = jnp.sum(passed.astype(jnp.int32), axis=1)
    starts = jnp.sum(jnp.where(passed, lengths[None, :], 0), axis=1)
    position = (row_ids - starts).astype(jnp.float32)
    half_width = head_width // 2
    frequency = rope_base ** (-(jnp.arange(half_width, dtype=jnp.float32) * 2.0 / head_width))
    angles = position[:, None] * frequency[None, :]
    valid_rows = (row_ids < seq_ends[-1]).astype(jnp.float32)
    return (jnp.cos(angles), jnp.sin(angles), segment, valid_rows)


def geglu(gate_up):
    hidden_units = gate_up.shape[-1] // 2
    return jax.nn.gelu(gate_up[:, :hidden_units], approximate=False) * gate_up[:, hidden_units:]


def nn(a, b):
    return jnp.dot(a, b, preferred_element_type=jnp.float32)


def nt(a, b):
    return lax.dot_general(a, b, (((1,), (1,)), ((), ())), preferred_element_type=jnp.float32)


def rotate(values, cos_wide, sin_wide):
    lane = lax.broadcasted_iota(jnp.int32, values.shape, 1)
    width = values.shape[1]
    swapped = jnp.where(
        (lane & 32) == 0, pltpu.roll(values, width - 32, 1), pltpu.roll(values, 32, 1)
    )
    return values * cos_wide + swapped * sin_wide


QB = 256


def attn_fwd_kernel(scale, a_ref, w_ref, cos_ref, sin_ref, segc_ref, segr_ref, qkv_ref, o_ref, lse_ref):
    rows = a_ref.shape[0]
    a1 = a_ref[...]
    cos_wide, sin_wide = cos_ref[...], sin_ref[...]
    q = rotate(nn(a1, w_ref[0]), cos_wide, sin_wide).astype(jnp.bfloat16)
    k = rotate(nn(a1, w_ref[1]), cos_wide, sin_wide).astype(jnp.bfloat16)
    v = nn(a1, w_ref[2])
    qkv_ref[0] = q
    qkv_ref[1] = k
    qkv_ref[2] = v.astype(jnp.bfloat16)
    v_t = jnp.transpose(v).astype(jnp.bfloat16)
    segc = segc_ref[...]
    ones = jnp.ones((16, rows), jnp.bfloat16)
    for b in range(rows // QB):
        qs = slice(b * QB, (b + 1) * QB)
        same = segc == segr_ref[:, qs]
        outs = []
        for h in range(2):
            hs = slice(h * 64, (h + 1) * 64)
            s_t = nt(k[:, hs], q[qs, hs]) * (scale * log2e)
            s_t = jnp.where(same, s_t, masked_score)
            top = jnp.max(s_t, axis=0, keepdims=True)
            e = jnp.exp2(s_t - top).astype(jnp.bfloat16)
            ov = nn(jnp.concatenate([v_t[hs], ones], axis=0), e)
            total = ov[64:65]
            outs.append(ov[:64] * (1.0 / total))
            lse_ref[0, h : h + 1, qs] = top + jnp.log2(total)
        o_ref[qs, :] = jnp.transpose(jnp.concatenate(outs, axis=0)).astype(jnp.bfloat16)


def attn_bwd_kernel(scale, qkv_ref, o_ref, go_ref, lse_ref, cos_ref, sin_ref, segc_ref, segr_ref, g_ref):
    rows = o_ref.shape[0]
    q, k, v, go = qkv_ref[0], qkv_ref[1], qkv_ref[2], go_ref[...]
    k_t = jnp.transpose(k.astype(jnp.float32)).astype(jnp.bfloat16)
    prod = jnp.transpose(go.astype(jnp.float32) * o_ref[...].astype(jnp.float32))
    segc = segc_ref[...]
    gk = [jnp.zeros((rows, 64), jnp.float32) for _ in range(2)]
    gv = [jnp.zeros((rows, 64), jnp.float32) for _ in range(2)]
    gq = []
    for b in range(rows // QB):
        qs = slice(b * QB, (b + 1) * QB)
        same = segc == segr_ref[:, qs]
        outs = []
        for h in range(2):
            hs = slice(h * 64, (h + 1) * 64)
            delta = jnp.sum(prod[hs, qs], axis=0, keepdims=True)
            s_t = nt(k[:, hs], q[qs, hs]) * (scale * log2e)
            p = jnp.exp2(jnp.where(same, s_t - lse_ref[0, h : h + 1, qs], masked_score))
            gp = nt(v[:, hs], go[qs, hs])
            gv[h] = gv[h] + nn(p.astype(jnp.bfloat16), go[qs, hs])
            ds = (p * (gp - delta)).astype(jnp.bfloat16)
            gk[h] = gk[h] + nn(ds, q[qs, hs])
            outs.append(nn(k_t[hs], ds))
        gq.append(jnp.transpose(jnp.concatenate(outs, axis=0)))
    cos_wide, sin_wide = cos_ref[...], sin_ref[...]
    gq = jnp.concatenate(gq, axis=0) * scale
    gk = jnp.concatenate(gk, axis=1) * scale
    g_ref[0] = rotate(gq, cos_wide, -sin_wide).astype(jnp.bfloat16)
    g_ref[1] = rotate(gk, cos_wide, -sin_wide).astype(jnp.bfloat16)
    g_ref[2] = jnp.concatenate(gv, axis=1).astype(jnp.bfloat16)


def whole_spec(shape):
    return pl.BlockSpec(shape, lambda i: tuple(0 for _ in shape))


def attn_forward(a1, w_qkv, cos_wide, sin_wide, segc, segr):
    rows, width = a1.shape
    pairs = HEADS // 2
    return pl.pallas_call(
        functools.partial(attn_fwd_kernel, (width // HEADS) ** (-0.5)),
        grid=(pairs,),
        in_specs=[
            whole_spec((rows, width)),
            pl.BlockSpec((3, width, 128), lambda i: (0, 0, i)),
            whole_spec((rows, 128)),
            whole_spec((rows, 128)),
            whole_spec((rows, 1)),
            whole_spec((1, rows)),
        ],
        out_specs=[
            pl.BlockSpec((3, rows, 128), lambda i: (0, 0, i)),
            pl.BlockSpec((rows, 128), lambda i: (0, i)),
            pl.BlockSpec((1, 2, rows), lambda i: (i, 0, 0)),
        ],
        out_shape=[
            jax.ShapeDtypeStruct((3, rows, width), jnp.bfloat16),
            jax.ShapeDtypeStruct((rows, width), jnp.bfloat16),
            jax.ShapeDtypeStruct((pairs, 2, rows), jnp.float32),
        ],
        compiler_params=pltpu.CompilerParams(vmem_limit_bytes=50 * MIB),
        cost_estimate=pl.CostEstimate(
            flops=2 * rows * rows * width * 2 + 6 * rows * width * width,
            bytes_accessed=20 * MIB,
            transcendentals=HEADS * rows * rows,
        ),
    )(a1, w_qkv, cos_wide, sin_wide, segc, segr)


def attn_backward(qkv, o, go, lse, cos_wide, sin_wide, segc, segr):
    rows, width = o.shape
    pairs = HEADS // 2
    pair_block = pl.BlockSpec((rows, 128), lambda i: (0, i))
    return pl.pallas_call(
        functools.partial(attn_bwd_kernel, (width // HEADS) ** (-0.5)),
        grid=(pairs,),
        in_specs=[
            pl.BlockSpec((3, rows, 128), lambda i: (0, 0, i)),
            pair_block,
            pair_block,
            pl.BlockSpec((1, 2, rows), lambda i: (i, 0, 0)),
            whole_spec((rows, 128)),
            whole_spec((rows, 128)),
            whole_spec((rows, 1)),
            whole_spec((1, rows)),
        ],
        out_specs=pl.BlockSpec((3, rows, 128), lambda i: (0, 0, i)),
        out_shape=jax.ShapeDtypeStruct((3, rows, width), jnp.bfloat16),
        compiler_params=pltpu.CompilerParams(vmem_limit_bytes=50 * MIB),
        cost_estimate=pl.CostEstimate(
            flops=2 * rows * rows * width * 5,
            bytes_accessed=20 * MIB,
            transcendentals=HEADS * rows * rows,
        ),
    )(qkv, o, go, lse, cos_wide, sin_wide, segc, segr)


def gather_weights(norm1_scale, qkv_weight, out_weight, norm2_scale, in_weight, mlp_out_weight):
    gather = functools.partial(lax.all_gather, axis_name="shard", axis=0, tiled=True)
    w_qkv = gather(qkv_weight)
    width = w_qkv.shape[0]
    w_qkv = w_qkv.reshape(width, 3, width).transpose(1, 0, 2)
    return (
        gather(norm1_scale),
        w_qkv,
        gather(out_weight),
        gather(norm2_scale),
        gather(in_weight),
        gather(mlp_out_weight),
    )


def reduce_grads(grads):
    def one(grad):
        part = lax.psum_scatter(
            grad.astype(jnp.bfloat16), "shard", scatter_dimension=0, tiled=True
        )
        return lax.psum(part, "rep").astype(jnp.float32)

    g1, gqkv, gout, g2, gin, gmlp = grads
    width = gout.shape[0]
    gqkv = gqkv.transpose(1, 0, 2).reshape(width, 3 * width)
    return tuple(one(item) for item in (g1, gqkv, gout, g2, gin, gmlp))


def per_device(
    hidden_in,
    seq_lengths,
    norm1_scale,
    qkv_weight,
    out_weight,
    norm2_scale,
    in_weight,
    mlp_out_weight,
    cotangent,
):
    token_rows, model_width = hidden_in.shape
    head_width = model_width // HEADS
    cosine, sine, segment, valid_rows = rotary_tables(seq_lengths[0], token_rows, head_width)
    cos_wide = jnp.concatenate([cosine] * 4, axis=1)
    sin_wide = jnp.concatenate([-sine, sine] * 2, axis=1)
    segc, segr = segment[:, None], segment[None, :]
    gain1, w_qkv, w_out, gain2, w_in, w_mlp = gather_weights(
        norm1_scale, qkv_weight, out_weight, norm2_scale, in_weight, mlp_out_weight
    )
    gain1, gain2 = gain1.astype(jnp.float32), gain2.astype(jnp.float32)
    inputs_f32 = hidden_in.astype(jnp.float32)
    normed_one, norm_one_back = jax.vjp(layer_norm, inputs_f32, gain1)
    normed_one = normed_one.astype(jnp.bfloat16)
    qkv, attn_low, lse = attn_forward(normed_one, w_qkv, cos_wide, sin_wide, segc, segr)
    resid_one = inputs_f32 + nn(attn_low, w_out)
    normed_two, norm_two_back = jax.vjp(layer_norm, resid_one, gain2)
    normed_two = normed_two.astype(jnp.bfloat16)
    gate_up = nn(normed_two, w_in)
    mixed, geglu_back = jax.vjp(geglu, gate_up)
    mixed_low = mixed.astype(jnp.bfloat16)
    output = (valid_rows[:, None] * (resid_one + nn(mixed_low, w_mlp))).astype(jnp.bfloat16)

    cot_rows = cotangent.astype(jnp.float32) * valid_rows[:, None]
    mlp_cot = cot_rows.astype(jnp.bfloat16)
    grad_mlp_out = jnp.einsum("nf,nd->fd", mixed_low, mlp_cot, preferred_element_type=jnp.float32)
    grad_mixed = nt(mlp_cot, w_mlp)
    grad_gate_up = geglu_back(grad_mixed)[0].astype(jnp.bfloat16)
    grad_in_w = jnp.einsum(
        "nd,nf->df", normed_two, grad_gate_up, preferred_element_type=jnp.float32
    )
    grad_normed_two = nt(grad_gate_up, w_in)
    grad_resid_ln, grad_gain_two = norm_two_back(grad_normed_two)
    grad_resid = cot_rows + grad_resid_ln
    attn_cot = grad_resid.astype(jnp.bfloat16)
    grad_out_w = jnp.einsum("nd,ne->de", attn_low, attn_cot, preferred_element_type=jnp.float32)
    grad_attn = nt(attn_cot, w_out).astype(jnp.bfloat16)
    grad_qkv = attn_backward(qkv, attn_low, grad_attn, lse, cos_wide, sin_wide, segc, segr)
    grad_qkv_w = jnp.einsum(
        "nd,cne->cde", normed_one, grad_qkv, preferred_element_type=jnp.float32
    )
    grad_normed_one = jnp.einsum(
        "cne,cde->nd", grad_qkv, w_qkv, preferred_element_type=jnp.float32
    )
    grad_input_ln, grad_gain_one = norm_one_back(grad_normed_one)
    input_grad = (grad_resid + grad_input_ln).astype(jnp.bfloat16)
    owned = reduce_grads(
        (grad_gain_one, grad_qkv_w, grad_out_w, grad_gain_two, grad_in_w, grad_mlp_out)
    )
    return (output, input_grad) + owned


def solution(mesh):
    rows = P(("rep", "shard"), None)
    weights = (P("shard"), P("shard", None), P("shard", None), P("shard"), P("shard", None), P("shard", None))
    return jax.shard_map(
        per_device,
        mesh=mesh,
        in_specs=(rows, rows) + weights + (rows,),
        out_specs=(rows, rows) + weights,
        check_vma=False,
    )
```

```python
import functools

import jax
import jax.numpy as jnp
from jax import lax
from jax.experimental import pallas as pl
from jax.experimental.pallas import tpu as pltpu
from jax.sharding import PartitionSpec as P

HEADS = 12


rope_base = 160000.0
norm_eps = 1e-05
masked_score = -1000000000.0
log2e = 1.4426950408889634
MIB = 1024 * 1024


def layer_norm(values, gain_vec):
    centered = values - jnp.mean(values, axis=-1, keepdims=True)
    spread = jnp.mean(centered * centered, axis=-1, keepdims=True)
    return centered * lax.rsqrt(spread + norm_eps) * gain_vec


def rotary_tables(lengths, token_rows, head_width):
    seq_ends = jnp.cumsum(lengths)
    row_ids = jnp.arange(token_rows, dtype=jnp.int32)
    passed = row_ids[:, None] >= seq_ends[None, :]
    segment = jnp.sum(passed.astype(jnp.int32), axis=1)
    starts = jnp.sum(jnp.where(passed, lengths[None, :], 0), axis=1)
    position = (row_ids - starts).astype(jnp.float32)
    half_width = head_width // 2
    frequency = rope_base ** (-(jnp.arange(half_width, dtype=jnp.float32) * 2.0 / head_width))
    angles = position[:, None] * frequency[None, :]
    valid_rows = (row_ids < seq_ends[-1]).astype(jnp.float32)
    return (jnp.cos(angles), jnp.sin(angles), segment, valid_rows)


def geglu(gate_up):
    hidden_units = gate_up.shape[-1] // 2
    return jax.nn.gelu(gate_up[:, :hidden_units], approximate=False) * gate_up[:, hidden_units:]


def nn(a, b):
    return jnp.dot(a, b, preferred_element_type=jnp.float32)


def nt(a, b):
    return lax.dot_general(a, b, (((1,), (1,)), ((), ())), preferred_element_type=jnp.float32)


def rotate(values, cos_wide, sin_wide):
    lane = lax.broadcasted_iota(jnp.int32, values.shape, 1)
    width = values.shape[1]
    swapped = jnp.where(
        (lane & 32) == 0, pltpu.roll(values, width - 32, 1), pltpu.roll(values, 32, 1)
    )
    return values * cos_wide + swapped * sin_wide


QB = 256


def attn_fwd_kernel(scale, a_ref, w_ref, cos_ref, sin_ref, segc_ref, segr_ref, qkv_ref, o_ref, lse_ref):
    rows = a_ref.shape[0]
    a1 = a_ref[...]
    cos_wide, sin_wide = cos_ref[...], sin_ref[...]
    q = rotate(nn(a1, w_ref[0]), cos_wide, sin_wide).astype(jnp.bfloat16)
    k = rotate(nn(a1, w_ref[1]), cos_wide, sin_wide).astype(jnp.bfloat16)
    v = nn(a1, w_ref[2])
    qkv_ref[0] = q
    qkv_ref[1] = k
    qkv_ref[2] = v.astype(jnp.bfloat16)
    v_t = jnp.transpose(v).astype(jnp.bfloat16)
    segc = segc_ref[...]
    ones = jnp.ones((16, rows), jnp.bfloat16)
    for b in range(rows // QB):
        qs = slice(b * QB, (b + 1) * QB)
        same = segc == segr_ref[:, qs]
        outs = []
        for h in range(2):
            hs = slice(h * 64, (h + 1) * 64)
            s_t = nt(k[:, hs], q[qs, hs]) * (scale * log2e)
            s_t = jnp.where(same, s_t, masked_score)
            top = jnp.max(s_t, axis=0, keepdims=True)
            e = jnp.exp2(s_t - top).astype(jnp.bfloat16)
            ov = nn(jnp.concatenate([v_t[hs], ones], axis=0), e)
            total = ov[64:65]
            outs.append(ov[:64] * (1.0 / total))
            lse_ref[0, h : h + 1, qs] = top + jnp.log2(total)
        o_ref[qs, :] = jnp.transpose(jnp.concatenate(outs, axis=0)).astype(jnp.bfloat16)


def attn_bwd_kernel(scale, qkv_ref, o_ref, go_ref, lse_ref, cos_ref, sin_ref, segc_ref, segr_ref, g_ref):
    rows = o_ref.shape[0]
    q, k, v, go = qkv_ref[0], qkv_ref[1], qkv_ref[2], go_ref[...]
    k_t = jnp.transpose(k.astype(jnp.float32)).astype(jnp.bfloat16)
    prod = jnp.transpose(go.astype(jnp.float32) * o_ref[...].astype(jnp.float32))
    segc = segc_ref[...]
    gk = [jnp.zeros((rows, 64), jnp.float32) for _ in range(2)]
    gv = [jnp.zeros((rows, 64), jnp.float32) for _ in range(2)]
    gq = []
    for b in range(rows // QB):
        qs = slice(b * QB, (b + 1) * QB)
        same = segc == segr_ref[:, qs]
        outs = []
        for h in range(2):
            hs = slice(h * 64, (h + 1) * 64)
            delta = jnp.sum(prod[hs, qs], axis=0, keepdims=True)
            s_t = nt(k[:, hs], q[qs, hs]) * (scale * log2e)
            p = jnp.exp2(jnp.where(same, s_t - lse_ref[0, h : h + 1, qs], masked_score))
            gp = nt(v[:, hs], go[qs, hs])
            gv[h] = gv[h] + nn(p.astype(jnp.bfloat16), go[qs, hs])
            ds = (p * (gp - delta)).astype(jnp.bfloat16)
            gk[h] = gk[h] + nn(ds, q[qs, hs])
            outs.append(nn(k_t[hs], ds))
        gq.append(jnp.transpose(jnp.concatenate(outs, axis=0)))
    cos_wide, sin_wide = cos_ref[...], sin_ref[...]
    gq = jnp.concatenate(gq, axis=0) * scale
    gk = jnp.concatenate(gk, axis=1) * scale
    g_ref[0] = rotate(gq, cos_wide, -sin_wide).astype(jnp.bfloat16)
    g_ref[1] = rotate(gk, cos_wide, -sin_wide).astype(jnp.bfloat16)
    g_ref[2] = jnp.concatenate(gv, axis=1).astype(jnp.bfloat16)


def whole_spec(shape):
    return pl.BlockSpec(shape, lambda i: tuple(0 for _ in shape))


def attn_forward(a1, w_qkv, cos_wide, sin_wide, segc, segr):
    rows, width = a1.shape
    pairs = HEADS // 2
    return pl.pallas_call(
        functools.partial(attn_fwd_kernel, (width // HEADS) ** (-0.5)),
        grid=(pairs,),
        in_specs=[
            whole_spec((rows, width)),
            pl.BlockSpec((3, width, 128), lambda i: (0, 0, i)),
            whole_spec((rows, 128)),
            whole_spec((rows, 128)),
            whole_spec((rows, 1)),
            whole_spec((1, rows)),
        ],
        out_specs=[
            pl.BlockSpec((3, rows, 128), lambda i: (0, 0, i)),
            pl.BlockSpec((rows, 128), lambda i: (0, i)),
            pl.BlockSpec((1, 2, rows), lambda i: (i, 0, 0)),
        ],
        out_shape=[
            jax.ShapeDtypeStruct((3, rows, width), jnp.bfloat16),
            jax.ShapeDtypeStruct((rows, width), jnp.bfloat16),
            jax.ShapeDtypeStruct((pairs, 2, rows), jnp.float32),
        ],
        compiler_params=pltpu.CompilerParams(vmem_limit_bytes=50 * MIB),
        cost_estimate=pl.CostEstimate(
            flops=2 * rows * rows * width * 2 + 6 * rows * width * width,
            bytes_accessed=20 * MIB,
            transcendentals=HEADS * rows * rows,
        ),
    )(a1, w_qkv, cos_wide, sin_wide, segc, segr)


def attn_backward(qkv, o, go, lse, cos_wide, sin_wide, segc, segr):
    rows, width = o.shape
    pairs = HEADS // 2
    pair_block = pl.BlockSpec((rows, 128), lambda i: (0, i))
    return pl.pallas_call(
        functools.partial(attn_bwd_kernel, (width // HEADS) ** (-0.5)),
        grid=(pairs,),
        in_specs=[
            pl.BlockSpec((3, rows, 128), lambda i: (0, 0, i)),
            pair_block,
            pair_block,
            pl.BlockSpec((1, 2, rows), lambda i: (i, 0, 0)),
            whole_spec((rows, 128)),
            whole_spec((rows, 128)),
            whole_spec((rows, 1)),
            whole_spec((1, rows)),
        ],
        out_specs=pl.BlockSpec((3, rows, 128), lambda i: (0, 0, i)),
        out_shape=jax.ShapeDtypeStruct((3, rows, width), jnp.bfloat16),
        compiler_params=pltpu.CompilerParams(vmem_limit_bytes=50 * MIB),
        cost_estimate=pl.CostEstimate(
            flops=2 * rows * rows * width * 5,
            bytes_accessed=20 * MIB,
            transcendentals=HEADS * rows * rows,
        ),
    )(qkv, o, go, lse, cos_wide, sin_wide, segc, segr)


def send_to(source, target, send_sem, recv_sem, peer):
    return pltpu.make_async_remote_copy(
        src_ref=source,
        dst_ref=target,
        send_sem=send_sem,
        recv_sem=recv_sem,
        device_id=peer,
        device_id_type=pl.DeviceIdType.MESH,
    )


def greet(peers):
    barrier = pltpu.get_barrier_semaphore()
    for peer in peers:
        pl.semaphore_signal(
            barrier, inc=1, device_id=peer, device_id_type=pl.DeviceIdType.MESH
        )
    pl.semaphore_wait(barrier, len(peers))


def rep_places():
    me = lax.axis_index("rep")
    sibling = me + 1 - 2 * lax.rem(me, 2)
    across = lax.rem(me + 2, 4)
    return me, sibling, across


def gather_kernel(shards, w_ref, out_ref, zs, zr, ys, yr, xs, xr):
    chunks = w_ref.shape[0]
    me_r, sibling, across = rep_places()
    me_s = lax.axis_index("shard")
    peers = [{"shard": lax.rem(me_s + d, shards)} for d in range(1, shards)]
    greet(peers + [{"rep": sibling}, {"rep": across}])
    ring = []
    for c in range(chunks):
        for d, peer in enumerate(peers):
            copy = send_to(
                w_ref.at[c, me_r], out_ref.at[c, me_r, me_s], zs.at[c, d], zr.at[c, d], peer
            )
            copy.start()
            ring.append(copy)
    for c in range(chunks):
        out_ref[c, me_r, me_s] = w_ref[c, me_r]
    acrosses, siblings = [], []

    def second(c):
        acrosses[c].wait_recv()
        copy = send_to(
            out_ref.at[c, across], out_ref.at[c, across], xs.at[c, 1], xr.at[c, 1], {"rep": sibling}
        )
        copy.start()
        siblings.append(copy)

    for c in range(chunks):
        for copy in ring[c * (shards - 1) : (c + 1) * (shards - 1)]:
            copy.wait_recv()
        part = out_ref.at[c, me_r]
        copy = send_to(part, part, ys.at[c], yr.at[c], {"rep": across})
        copy.start()
        acrosses.append(copy)
        copy = send_to(part, part, xs.at[c, 0], xr.at[c, 0], {"rep": sibling})
        copy.start()
        siblings.append(copy)
        if c >= 1:
            second(c - 1)
    second(chunks - 1)
    for copy in siblings:
        copy.wait_recv()
    for copy in ring + acrosses + siblings:
        copy.wait_send()


def gather_call(packed, shards, collective_id):
    chunks, reps, rows, lanes = packed.shape
    return pl.pallas_call(
        functools.partial(gather_kernel, shards),
        out_shape=jax.ShapeDtypeStruct((chunks, reps, shards, rows, lanes), packed.dtype),
        in_specs=[pl.BlockSpec(memory_space=pltpu.VMEM)],
        out_specs=pl.BlockSpec(memory_space=pltpu.VMEM),
        scratch_shapes=[
            pltpu.SemaphoreType.DMA((chunks, shards - 1)),
            pltpu.SemaphoreType.DMA((chunks, shards - 1)),
            pltpu.SemaphoreType.DMA((chunks,)),
            pltpu.SemaphoreType.DMA((chunks,)),
            pltpu.SemaphoreType.DMA((chunks, 2)),
            pltpu.SemaphoreType.DMA((chunks, 2)),
        ],
        compiler_params=pltpu.CompilerParams(
            collective_id=collective_id, has_side_effects=True, vmem_limit_bytes=50 * MIB
        ),
    )(packed)


def reduce_kernel(
    g_ref, out_ref, ra, t, rb, u, rc, rd, a_s, a_r, b_s, b_r, c_s, c_r, d_s, d_r
):
    chunks, reps, shards = g_ref.shape[:3]
    me_r, sibling, across = rep_places()
    sib_across = lax.rem(sibling + 2, 4)
    me_s = lax.axis_index("shard")
    places = [lax.rem(me_s + d, shards) for d in range(1, shards)]
    others = [lax.rem(me_r + d, reps) for d in range(1, reps)]
    greet([{"shard": place} for place in places] + [{"rep": place} for place in others])
    low, wide = g_ref.dtype, jnp.float32
    a, b, cc, dd = {}, [], {}, {}
    for c in range(chunks):
        for j, quarter in enumerate((sib_across, sibling)):
            a[c, j] = send_to(
                g_ref.at[c, quarter], ra.at[c, j], a_s.at[c, j], a_r.at[c, j], {"rep": sibling}
            )
            a[c, j].start()

    def stage_b(c):
        a[c, 0].wait_recv()

        def add(j, carry):
            t[c, j] = (g_ref[c, across, j].astype(wide) + ra[c, 0, j].astype(wide)).astype(low)
            return carry

        lax.fori_loop(0, shards, add, 0)
        copy = send_to(t.at[c], rb.at[c], b_s.at[c], b_r.at[c], {"rep": across})
        copy.start()
        b.append(copy)

    def stage_c(c):
        a[c, 1].wait_recv()
        b[c].wait_recv()

        def add(j, carry):
            u[c, j] = (
                g_ref[c, me_r, j].astype(wide) + ra[c, 1, j].astype(wide) + rb[c, j].astype(wide)
            ).astype(low)
            return carry

        lax.fori_loop(0, shards, add, 0)
        for d, place in enumerate(places):
            cc[c, d] = send_to(
                u.at[c, place], rc.at[c, d], c_s.at[c, d], c_r.at[c, d], {"shard": place}
            )
            cc[c, d].start()

    def stage_d(c):
        for d in range(shards - 1):
            cc[c, d].wait_recv()

        def add(j, total):
            return total + rc[c, j].astype(wide)

        total = lax.fori_loop(0, shards - 1, add, u[c, me_s].astype(wide))
        rd[c, me_r] = total.astype(low)
        for d, place in enumerate(others):
            dd[c, d] = send_to(
                rd.at[c, me_r], rd.at[c, me_r], d_s.at[c, d], d_r.at[c, d], {"rep": place}
            )
            dd[c, d].start()

    stage_b(0)
    for c in range(chunks):
        if c + 1 < chunks:
            stage_b(c + 1)
        stage_c(c)
        if c >= 1:
            stage_d(c - 1)
    stage_d(chunks - 1)
    for copy in list(dd.values()):
        copy.wait_recv()
    for copy in list(a.values()) + b + list(cc.values()) + list(dd.values()):
        copy.wait_send()
    for c in range(chunks):
        for r in range(reps):
            out_ref[c, r] = rd[c, r].astype(out_ref.dtype)


def reduce_call(packed, collective_id):
    chunks, reps, shards, rows, lanes = packed.shape
    low, sems = packed.dtype, pltpu.SemaphoreType.DMA
    return pl.pallas_call(
        reduce_kernel,
        out_shape=jax.ShapeDtypeStruct((chunks, reps, rows, lanes), jnp.float32),
        in_specs=[pl.BlockSpec(memory_space=pltpu.VMEM)],
        out_specs=pl.BlockSpec(memory_space=pltpu.VMEM),
        scratch_shapes=[
            pltpu.VMEM((chunks, 2, shards, rows, lanes), low),
            pltpu.VMEM((chunks, shards, rows, lanes), low),
            pltpu.VMEM((chunks, shards, rows, lanes), low),
            pltpu.VMEM((chunks, shards, rows, lanes), low),
            pltpu.VMEM((chunks, shards - 1, rows, lanes), low),
            pltpu.VMEM((chunks, reps, rows, lanes), low),
            sems((chunks, 2)),
            sems((chunks, 2)),
            sems((chunks,)),
            sems((chunks,)),
            sems((chunks, shards - 1)),
            sems((chunks, shards - 1)),
            sems((chunks, reps - 1)),
            sems((chunks, reps - 1)),
        ],
        compiler_params=pltpu.CompilerParams(
            collective_id=collective_id, has_side_effects=True, vmem_limit_bytes=50 * MIB
        ),
    )(packed)


CHUNKS = 3


def can_use_kernels(width, hidden):
    shards = lax.axis_size("shard")
    rows = (7 * width + hidden) // shards
    return (
        lax.axis_size("rep") == 4
        and width % (128 * CHUNKS) == 0
        and width % shards == 0
        and hidden % shards == 0
        and rows % 16 == 0
    )


def padded_rows(width, hidden):
    rows = (7 * width + hidden) // lax.axis_size("shard") + 2
    return -(-rows // 64) * 64


def by_thirds(weight, shards, width):
    n, parts = weight.shape[0] // shards, weight.shape[1] // width
    return weight.reshape(shards, n, parts, width).transpose(0, 2, 1, 3).reshape(
        shards, parts * n, width
    )


def pack(norm1, qkv, out, norm2, into, mlp, rows):
    shards, _, width = out.shape
    norms = jnp.stack([norm1, norm2], axis=1)
    used = qkv.shape[1] + into.shape[1] + out.shape[1] + mlp.shape[1]
    norms = jnp.pad(norms, ((0, 0), (0, rows - used - 2), (0, width - norms.shape[2])))
    return jnp.concatenate([qkv, into, out, mlp, norms], axis=1)


def unpack(packed, n, hidden_n):
    at = [3 * n, 6 * n, 7 * n, 7 * n + hidden_n]
    qkv, into, out, mlp = (
        packed[:, lo:hi] for lo, hi in zip([0] + at[:-1], at)
    )
    return packed[:, at[3], :n], qkv, out, packed[:, at[3] + 1, :n], into, mlp


def gather_weights(norm1_scale, qkv_weight, out_weight, norm2_scale, in_weight, mlp_out_weight):
    n, width = out_weight.shape
    hidden_n = mlp_out_weight.shape[0]
    shards = lax.axis_size("shard")
    hidden = hidden_n * shards
    if not can_use_kernels(width, hidden):
        gather = functools.partial(lax.all_gather, axis_name="shard", axis=0, tiled=True)
        return (
            gather(norm1_scale),
            gather(qkv_weight).reshape(width, 3, width).transpose(1, 0, 2),
            gather(out_weight),
            gather(norm2_scale),
            gather(in_weight),
            gather(mlp_out_weight),
        )
    rows = padded_rows(width, hidden)
    reps = lax.axis_size("rep")
    packed = pack(
        norm1_scale[None],
        by_thirds(qkv_weight, 1, width),
        out_weight[None],
        norm2_scale[None],
        by_thirds(in_weight, 1, width),
        mlp_out_weight[None],
        rows,
    )
    packed = packed.reshape(reps, rows // reps, CHUNKS, width // CHUNKS).transpose(2, 0, 1, 3)
    everything = gather_call(packed, shards, 0)
    everything = everything.transpose(2, 1, 3, 0, 4).reshape(shards, rows, width)
    norm1, qkv, out, norm2, into, mlp = unpack(everything, n, hidden_n)
    return (
        norm1.reshape(width),
        qkv.reshape(shards, 3, n, width).transpose(1, 0, 2, 3).reshape(3, width, width),
        out.reshape(width, width),
        norm2.reshape(width),
        into.reshape(shards, 3, n, width).transpose(0, 2, 1, 3).reshape(width, 3 * width),
        mlp.reshape(hidden, width),
    )


def reduce_grads(grads):
    g1, gqkv, gout, g2, gin, gmlp = (item.astype(jnp.bfloat16) for item in grads)
    width, hidden = gout.shape[0], gmlp.shape[0]
    shards, reps = lax.axis_size("shard"), lax.axis_size("rep")
    n, hidden_n = width // shards, hidden // shards
    if not can_use_kernels(width, hidden):

        def one(grad):
            part = lax.psum_scatter(grad, "shard", scatter_dimension=0, tiled=True)
            return lax.psum(part, "rep").astype(jnp.float32)

        gqkv = gqkv.transpose(1, 0, 2).reshape(width, 3 * width)
        return tuple(one(item) for item in (g1, gqkv, gout, g2, gin, gmlp))
    rows = padded_rows(width, hidden)
    packed = pack(
        g1.reshape(shards, n),
        gqkv.reshape(3, shards, n, width).transpose(1, 0, 2, 3).reshape(shards, 3 * n, width),
        gout.reshape(shards, n, width),
        g2.reshape(shards, n),
        by_thirds(gin, shards, width),
        gmlp.reshape(shards, hidden_n, width),
        rows,
    )
    packed = packed.reshape(shards, reps, rows // reps, CHUNKS, width // CHUNKS)
    owned = reduce_call(packed.transpose(3, 1, 0, 2, 4), 1)
    owned = owned.transpose(1, 2, 0, 3).reshape(1, rows, width)
    norm1, qkv, out, norm2, into, mlp = unpack(owned, n, hidden_n)
    wide = [
        item.reshape(3, n, width).transpose(1, 0, 2).reshape(n, 3 * width) for item in (qkv, into)
    ]
    return (norm1[0], wide[0], out[0], norm2[0], wide[1], mlp[0])


def per_device(
    hidden_in,
    seq_lengths,
    norm1_scale,
    qkv_weight,
    out_weight,
    norm2_scale,
    in_weight,
    mlp_out_weight,
    cotangent,
):
    token_rows, model_width = hidden_in.shape
    head_width = model_width // HEADS
    cosine, sine, segment, valid_rows = rotary_tables(seq_lengths[0], token_rows, head_width)
    cos_wide = jnp.concatenate([cosine] * 4, axis=1)
    sin_wide = jnp.concatenate([-sine, sine] * 2, axis=1)
    segc, segr = segment[:, None], segment[None, :]
    gain1, w_qkv, w_out, gain2, w_in, w_mlp = gather_weights(
        norm1_scale, qkv_weight, out_weight, norm2_scale, in_weight, mlp_out_weight
    )
    gain1, gain2 = gain1.astype(jnp.float32), gain2.astype(jnp.float32)
    inputs_f32 = hidden_in.astype(jnp.float32)
    normed_one, norm_one_back = jax.vjp(layer_norm, inputs_f32, gain1)
    normed_one = normed_one.astype(jnp.bfloat16)
    qkv, attn_low, lse = attn_forward(normed_one, w_qkv, cos_wide, sin_wide, segc, segr)
    resid_one = inputs_f32 + nn(attn_low, w_out)
    normed_two, norm_two_back = jax.vjp(layer_norm, resid_one, gain2)
    normed_two = normed_two.astype(jnp.bfloat16)
    gate_up = nn(normed_two, w_in)
    mixed, geglu_back = jax.vjp(geglu, gate_up)
    mixed_low = mixed.astype(jnp.bfloat16)
    output = (valid_rows[:, None] * (resid_one + nn(mixed_low, w_mlp))).astype(jnp.bfloat16)

    cot_rows = cotangent.astype(jnp.float32) * valid_rows[:, None]
    mlp_cot = cot_rows.astype(jnp.bfloat16)
    grad_mlp_out = jnp.einsum("nf,nd->fd", mixed_low, mlp_cot, preferred_element_type=jnp.float32)
    grad_mixed = nt(mlp_cot, w_mlp)
    grad_gate_up = geglu_back(grad_mixed)[0].astype(jnp.bfloat16)
    grad_in_w = jnp.einsum(
        "nd,nf->df", normed_two, grad_gate_up, preferred_element_type=jnp.float32
    )
    grad_normed_two = nt(grad_gate_up, w_in)
    grad_resid_ln, grad_gain_two = norm_two_back(grad_normed_two)
    grad_resid = cot_rows + grad_resid_ln
    attn_cot = grad_resid.astype(jnp.bfloat16)
    grad_out_w = jnp.einsum("nd,ne->de", attn_low, attn_cot, preferred_element_type=jnp.float32)
    grad_attn = nt(attn_cot, w_out).astype(jnp.bfloat16)
    grad_qkv = attn_backward(qkv, attn_low, grad_attn, lse, cos_wide, sin_wide, segc, segr)
    grad_qkv_w = jnp.einsum(
        "nd,cne->cde", normed_one, grad_qkv, preferred_element_type=jnp.float32
    )
    grad_normed_one = jnp.einsum(
        "cne,cde->nd", grad_qkv, w_qkv, preferred_element_type=jnp.float32
    )
    grad_input_ln, grad_gain_one = norm_one_back(grad_normed_one)
    input_grad = (grad_resid + grad_input_ln).astype(jnp.bfloat16)
    owned = reduce_grads(
        (grad_gain_one, grad_qkv_w, grad_out_w, grad_gain_two, grad_in_w, grad_mlp_out)
    )
    return (output, input_grad) + owned


def solution(mesh):
    rows = P(("rep", "shard"), None)
    weights = (P("shard"), P("shard", None), P("shard", None), P("shard"), P("shard", None), P("shard", None))
    return jax.shard_map(
        per_device,
        mesh=mesh,
        in_specs=(rows, rows) + weights + (rows,),
        out_specs=(rows, rows) + weights,
        check_vma=False,
    )
```

```python
import functools

import jax
import jax.numpy as jnp
from jax import lax
from jax.experimental import pallas as pl
from jax.experimental.pallas import tpu as pltpu
from jax.sharding import PartitionSpec as P

HEADS = 12


rope_base = 160000.0
norm_eps = 1e-05
masked_score = -1000000000.0
log2e = 1.4426950408889634
MIB = 1024 * 1024


def layer_norm(values, gain_vec):
    centered = values - jnp.mean(values, axis=-1, keepdims=True)
    spread = jnp.mean(centered * centered, axis=-1, keepdims=True)
    return centered * lax.rsqrt(spread + norm_eps) * gain_vec


def rotary_tables(lengths, token_rows, head_width):
    seq_ends = jnp.cumsum(lengths)
    row_ids = jnp.arange(token_rows, dtype=jnp.int32)
    passed = row_ids[:, None] >= seq_ends[None, :]
    segment = jnp.sum(passed.astype(jnp.int32), axis=1)
    starts = jnp.sum(jnp.where(passed, lengths[None, :], 0), axis=1)
    position = (row_ids - starts).astype(jnp.float32)
    half_width = head_width // 2
    frequency = rope_base ** (-(jnp.arange(half_width, dtype=jnp.float32) * 2.0 / head_width))
    angles = position[:, None] * frequency[None, :]
    valid_rows = (row_ids < seq_ends[-1]).astype(jnp.float32)
    return (jnp.cos(angles), jnp.sin(angles), segment, valid_rows)


def geglu(gate_up):
    hidden_units = gate_up.shape[-1] // 2
    return jax.nn.gelu(gate_up[:, :hidden_units], approximate=False) * gate_up[:, hidden_units:]


def nn(a, b):
    return jnp.dot(a, b, preferred_element_type=jnp.float32)


def nt(a, b):
    return lax.dot_general(a, b, (((1,), (1,)), ((), ())), preferred_element_type=jnp.float32)


def rotate(values, cos_wide, sin_wide):
    lane = lax.broadcasted_iota(jnp.int32, values.shape, 1)
    width = values.shape[1]
    swapped = jnp.where(
        (lane & 32) == 0, pltpu.roll(values, width - 32, 1), pltpu.roll(values, 32, 1)
    )
    return values * cos_wide + swapped * sin_wide


QB = 256


def attn_fwd_kernel(scale, a_ref, w_ref, cos_ref, sin_ref, segc_ref, segr_ref, qkv_ref, o_ref, lse_ref):
    rows = a_ref.shape[0]
    a1 = a_ref[...]
    cos_wide, sin_wide = cos_ref[...], sin_ref[...]
    q = rotate(nn(a1, w_ref[0]), cos_wide, sin_wide).astype(jnp.bfloat16)
    k = rotate(nn(a1, w_ref[1]), cos_wide, sin_wide).astype(jnp.bfloat16)
    v = nn(a1, w_ref[2])
    qkv_ref[0] = q
    qkv_ref[1] = k
    qkv_ref[2] = v.astype(jnp.bfloat16)
    v_t = jnp.transpose(v).astype(jnp.bfloat16)
    segc = segc_ref[...]
    ones = jnp.ones((16, rows), jnp.bfloat16)
    for b in range(rows // QB):
        qs = slice(b * QB, (b + 1) * QB)
        same = segc == segr_ref[:, qs]
        outs = []
        for h in range(2):
            hs = slice(h * 64, (h + 1) * 64)
            s_t = nt(k[:, hs], q[qs, hs]) * (scale * log2e)
            s_t = jnp.where(same, s_t, masked_score)
            top = jnp.max(s_t, axis=0, keepdims=True)
            e = jnp.exp2(s_t - top).astype(jnp.bfloat16)
            ov = nn(jnp.concatenate([v_t[hs], ones], axis=0), e)
            total = ov[64:65]
            outs.append(ov[:64] * (1.0 / total))
            lse_ref[0, h : h + 1, qs] = top + jnp.log2(total)
        o_ref[qs, :] = jnp.transpose(jnp.concatenate(outs, axis=0)).astype(jnp.bfloat16)


def attn_bwd_kernel(scale, qkv_ref, o_ref, go_ref, lse_ref, cos_ref, sin_ref, segc_ref, segr_ref, g_ref):
    rows = o_ref.shape[0]
    q, k, v, go = qkv_ref[0], qkv_ref[1], qkv_ref[2], go_ref[...]
    k_t = jnp.transpose(k.astype(jnp.float32)).astype(jnp.bfloat16)
    prod = jnp.transpose(go.astype(jnp.float32) * o_ref[...].astype(jnp.float32))
    segc = segc_ref[...]
    gk = [jnp.zeros((rows, 64), jnp.float32) for _ in range(2)]
    gv = [jnp.zeros((rows, 64), jnp.float32) for _ in range(2)]
    gq = []
    for b in range(rows // QB):
        qs = slice(b * QB, (b + 1) * QB)
        same = segc == segr_ref[:, qs]
        outs = []
        for h in range(2):
            hs = slice(h * 64, (h + 1) * 64)
            delta = jnp.sum(prod[hs, qs], axis=0, keepdims=True)
            s_t = nt(k[:, hs], q[qs, hs]) * (scale * log2e)
            p = jnp.exp2(jnp.where(same, s_t - lse_ref[0, h : h + 1, qs], masked_score))
            gp = nt(v[:, hs], go[qs, hs])
            gv[h] = gv[h] + nn(p.astype(jnp.bfloat16), go[qs, hs])
            ds = (p * (gp - delta)).astype(jnp.bfloat16)
            gk[h] = gk[h] + nn(ds, q[qs, hs])
            outs.append(nn(k_t[hs], ds))
        gq.append(jnp.transpose(jnp.concatenate(outs, axis=0)))
    cos_wide, sin_wide = cos_ref[...], sin_ref[...]
    gq = jnp.concatenate(gq, axis=0) * scale
    gk = jnp.concatenate(gk, axis=1) * scale
    g_ref[0] = rotate(gq, cos_wide, -sin_wide).astype(jnp.bfloat16)
    g_ref[1] = rotate(gk, cos_wide, -sin_wide).astype(jnp.bfloat16)
    g_ref[2] = jnp.concatenate(gv, axis=1).astype(jnp.bfloat16)


def whole_spec(shape):
    return pl.BlockSpec(shape, lambda i: tuple(0 for _ in shape))


def attn_forward(a1, w_qkv, cos_wide, sin_wide, segc, segr):
    rows, width = a1.shape
    pairs = HEADS // 2
    return pl.pallas_call(
        functools.partial(attn_fwd_kernel, (width // HEADS) ** (-0.5)),
        grid=(pairs,),
        in_specs=[
            whole_spec((rows, width)),
            pl.BlockSpec((3, width, 128), lambda i: (0, 0, i)),
            whole_spec((rows, 128)),
            whole_spec((rows, 128)),
            whole_spec((rows, 1)),
            whole_spec((1, rows)),
        ],
        out_specs=[
            pl.BlockSpec((3, rows, 128), lambda i: (0, 0, i)),
            pl.BlockSpec((rows, 128), lambda i: (0, i)),
            pl.BlockSpec((1, 2, rows), lambda i: (i, 0, 0)),
        ],
        out_shape=[
            jax.ShapeDtypeStruct((3, rows, width), jnp.bfloat16),
            jax.ShapeDtypeStruct((rows, width), jnp.bfloat16),
            jax.ShapeDtypeStruct((pairs, 2, rows), jnp.float32),
        ],
        compiler_params=pltpu.CompilerParams(vmem_limit_bytes=50 * MIB),
        cost_estimate=pl.CostEstimate(
            flops=2 * rows * rows * width * 2 + 6 * rows * width * width,
            bytes_accessed=20 * MIB,
            transcendentals=HEADS * rows * rows,
        ),
    )(a1, w_qkv, cos_wide, sin_wide, segc, segr)


def attn_backward(qkv, o, go, lse, cos_wide, sin_wide, segc, segr):
    rows, width = o.shape
    pairs = HEADS // 2
    pair_block = pl.BlockSpec((rows, 128), lambda i: (0, i))
    return pl.pallas_call(
        functools.partial(attn_bwd_kernel, (width // HEADS) ** (-0.5)),
        grid=(pairs,),
        in_specs=[
            pl.BlockSpec((3, rows, 128), lambda i: (0, 0, i)),
            pair_block,
            pair_block,
            pl.BlockSpec((1, 2, rows), lambda i: (i, 0, 0)),
            whole_spec((rows, 128)),
            whole_spec((rows, 128)),
            whole_spec((rows, 1)),
            whole_spec((1, rows)),
        ],
        out_specs=pl.BlockSpec((3, rows, 128), lambda i: (0, 0, i)),
        out_shape=jax.ShapeDtypeStruct((3, rows, width), jnp.bfloat16),
        compiler_params=pltpu.CompilerParams(vmem_limit_bytes=50 * MIB),
        cost_estimate=pl.CostEstimate(
            flops=2 * rows * rows * width * 5,
            bytes_accessed=20 * MIB,
            transcendentals=HEADS * rows * rows,
        ),
    )(qkv, o, go, lse, cos_wide, sin_wide, segc, segr)


def send_to(source, target, send_sem, recv_sem, peer):
    return pltpu.make_async_remote_copy(
        src_ref=source,
        dst_ref=target,
        send_sem=send_sem,
        recv_sem=recv_sem,
        device_id=peer,
        device_id_type=pl.DeviceIdType.MESH,
    )


def greet(peers):
    barrier = pltpu.get_barrier_semaphore()
    for peer in peers:
        pl.semaphore_signal(
            barrier, inc=1, device_id=peer, device_id_type=pl.DeviceIdType.MESH
        )
    pl.semaphore_wait(barrier, len(peers))


def rep_places():
    me = lax.axis_index("rep")
    sibling = me + 1 - 2 * lax.rem(me, 2)
    across = lax.rem(me + 2, 4)
    return me, sibling, across


def gather_kernel(shards, w_ref, out_ref, zs, zr, ys, yr, xs, xr):
    chunks = w_ref.shape[0]
    me_r, sibling, across = rep_places()
    me_s = lax.axis_index("shard")
    peers = [{"shard": lax.rem(me_s + d, shards)} for d in range(1, shards)]
    greet(peers + [{"rep": sibling}, {"rep": across}])
    ring = []
    for c in range(chunks):
        for d, peer in enumerate(peers):
            copy = send_to(
                w_ref.at[c, me_r], out_ref.at[c, me_r, me_s], zs.at[c, d], zr.at[c, d], peer
            )
            copy.start()
            ring.append(copy)
    for c in range(chunks):
        out_ref[c, me_r, me_s] = w_ref[c, me_r]
    acrosses, siblings = [], []

    def second(c):
        acrosses[c].wait_recv()
        copy = send_to(
            out_ref.at[c, across], out_ref.at[c, across], xs.at[c, 1], xr.at[c, 1], {"rep": sibling}
        )
        copy.start()
        siblings.append(copy)

    for c in range(chunks):
        for copy in ring[c * (shards - 1) : (c + 1) * (shards - 1)]:
            copy.wait_recv()
        part = out_ref.at[c, me_r]
        copy = send_to(part, part, ys.at[c], yr.at[c], {"rep": across})
        copy.start()
        acrosses.append(copy)
        copy = send_to(part, part, xs.at[c, 0], xr.at[c, 0], {"rep": sibling})
        copy.start()
        siblings.append(copy)
        if c >= 1:
            second(c - 1)
    second(chunks - 1)
    for copy in siblings:
        copy.wait_recv()
    for copy in ring + acrosses + siblings:
        copy.wait_send()


def gather_call(packed, shards, collective_id):
    chunks, reps, rows, lanes = packed.shape
    return pl.pallas_call(
        functools.partial(gather_kernel, shards),
        out_shape=jax.ShapeDtypeStruct((chunks, reps, shards, rows, lanes), packed.dtype),
        in_specs=[pl.BlockSpec(memory_space=pltpu.VMEM)],
        out_specs=pl.BlockSpec(memory_space=pltpu.VMEM),
        scratch_shapes=[
            pltpu.SemaphoreType.DMA((chunks, shards - 1)),
            pltpu.SemaphoreType.DMA((chunks, shards - 1)),
            pltpu.SemaphoreType.DMA((chunks,)),
            pltpu.SemaphoreType.DMA((chunks,)),
            pltpu.SemaphoreType.DMA((chunks, 2)),
            pltpu.SemaphoreType.DMA((chunks, 2)),
        ],
        compiler_params=pltpu.CompilerParams(
            collective_id=collective_id, has_side_effects=True, vmem_limit_bytes=50 * MIB
        ),
    )(packed)


def reduce_kernel(
    g_ref, out_ref, ra, t, rb, u, rc, rd, a_s, a_r, b_s, b_r, c_s, c_r, d_s, d_r
):
    chunks, reps, shards = g_ref.shape[:3]
    me_r, sibling, across = rep_places()
    sib_across = lax.rem(sibling + 2, 4)
    me_s = lax.axis_index("shard")
    places = [lax.rem(me_s + d, shards) for d in range(1, shards)]
    others = [lax.rem(me_r + d, reps) for d in range(1, reps)]
    greet([{"shard": place} for place in places] + [{"rep": place} for place in others])
    low, wide = g_ref.dtype, jnp.float32
    a, b, cc, dd = {}, [], {}, {}
    for c in range(chunks):
        for j, quarter in enumerate((sib_across, sibling)):
            a[c, j] = send_to(
                g_ref.at[c, quarter], ra.at[c, j], a_s.at[c, j], a_r.at[c, j], {"rep": sibling}
            )
            a[c, j].start()

    def stage_b(c):
        a[c, 0].wait_recv()

        def add(j, carry):
            t[c, j] = (g_ref[c, across, j].astype(wide) + ra[c, 0, j].astype(wide)).astype(low)
            return carry

        lax.fori_loop(0, shards, add, 0)
        copy = send_to(t.at[c], rb.at[c], b_s.at[c], b_r.at[c], {"rep": across})
        copy.start()
        b.append(copy)

    def stage_c(c):
        a[c, 1].wait_recv()
        b[c].wait_recv()

        def add(j, carry):
            u[c, j] = (
                g_ref[c, me_r, j].astype(wide) + ra[c, 1, j].astype(wide) + rb[c, j].astype(wide)
            ).astype(low)
            return carry

        lax.fori_loop(0, shards, add, 0)
        for d, place in enumerate(places):
            cc[c, d] = send_to(
                u.at[c, place], rc.at[c, d], c_s.at[c, d], c_r.at[c, d], {"shard": place}
            )
            cc[c, d].start()

    def stage_d(c):
        for d in range(shards - 1):
            cc[c, d].wait_recv()

        def add(j, total):
            return total + rc[c, j].astype(wide)

        total = lax.fori_loop(0, shards - 1, add, u[c, me_s].astype(wide))
        rd[c, me_r] = total.astype(low)
        for d, place in enumerate(others):
            dd[c, d] = send_to(
                rd.at[c, me_r], rd.at[c, me_r], d_s.at[c, d], d_r.at[c, d], {"rep": place}
            )
            dd[c, d].start()

    stage_b(0)
    for c in range(chunks):
        if c + 1 < chunks:
            stage_b(c + 1)
        stage_c(c)
        if c >= 1:
            stage_d(c - 1)
    stage_d(chunks - 1)
    for copy in list(dd.values()):
        copy.wait_recv()
    for copy in list(a.values()) + b + list(cc.values()) + list(dd.values()):
        copy.wait_send()
    for c in range(chunks):
        for r in range(reps):
            out_ref[c, r] = rd[c, r].astype(out_ref.dtype)


def reduce_call(packed, collective_id):
    chunks, reps, shards, rows, lanes = packed.shape
    low, sems = packed.dtype, pltpu.SemaphoreType.DMA
    return pl.pallas_call(
        reduce_kernel,
        out_shape=jax.ShapeDtypeStruct((chunks, reps, rows, lanes), jnp.float32),
        in_specs=[pl.BlockSpec(memory_space=pltpu.VMEM)],
        out_specs=pl.BlockSpec(memory_space=pltpu.VMEM),
        scratch_shapes=[
            pltpu.VMEM((chunks, 2, shards, rows, lanes), low),
            pltpu.VMEM((chunks, shards, rows, lanes), low),
            pltpu.VMEM((chunks, shards, rows, lanes), low),
            pltpu.VMEM((chunks, shards, rows, lanes), low),
            pltpu.VMEM((chunks, shards - 1, rows, lanes), low),
            pltpu.VMEM((chunks, reps, rows, lanes), low),
            sems((chunks, 2)),
            sems((chunks, 2)),
            sems((chunks,)),
            sems((chunks,)),
            sems((chunks, shards - 1)),
            sems((chunks, shards - 1)),
            sems((chunks, reps - 1)),
            sems((chunks, reps - 1)),
        ],
        compiler_params=pltpu.CompilerParams(
            collective_id=collective_id, has_side_effects=True, vmem_limit_bytes=50 * MIB
        ),
    )(packed)


CHUNKS = 3


def can_use_kernels(width, hidden):
    shards = lax.axis_size("shard")
    rows = (7 * width + hidden) // shards
    return (
        lax.axis_size("rep") == 4
        and width % (128 * CHUNKS) == 0
        and width % shards == 0
        and hidden % shards == 0
        and rows % 16 == 0
    )


def padded_rows(width, hidden):
    rows = (7 * width + hidden) // lax.axis_size("shard") + 2
    return -(-rows // 64) * 64


def by_thirds(weight, shards, width):
    n, parts = weight.shape[0] // shards, weight.shape[1] // width
    weight = weight.reshape(shards, n, parts * width)
    return jnp.concatenate(
        [weight[:, :, p * width : (p + 1) * width] for p in range(parts)], axis=1
    )


def lane_chunks(values):
    lanes = values.shape[-1] // CHUNKS
    return jnp.stack([values[..., c * lanes : (c + 1) * lanes] for c in range(CHUNKS)])


def join_lanes(pieces):
    return jnp.concatenate([pieces[i] for i in range(pieces.shape[0])], axis=-1)


def pack(norm1, qkv, out, norm2, into, mlp, rows):
    shards, _, width = out.shape
    norms = jnp.stack([norm1, norm2], axis=1)
    used = qkv.shape[1] + into.shape[1] + out.shape[1] + mlp.shape[1]
    norms = jnp.pad(norms, ((0, 0), (0, rows - used - 2), (0, width - norms.shape[2])))
    return jnp.concatenate([qkv, into, out, mlp, norms], axis=1)


def unpack(packed, n, hidden_n):
    at = [3 * n, 6 * n, 7 * n, 7 * n + hidden_n]
    qkv, into, out, mlp = (
        packed[:, lo:hi] for lo, hi in zip([0] + at[:-1], at)
    )
    return packed[:, at[3], :n], qkv, out, packed[:, at[3] + 1, :n], into, mlp


def gather_weights(norm1_scale, qkv_weight, out_weight, norm2_scale, in_weight, mlp_out_weight):
    n, width = out_weight.shape
    hidden_n = mlp_out_weight.shape[0]
    shards = lax.axis_size("shard")
    hidden = hidden_n * shards
    if not can_use_kernels(width, hidden):
        gather = functools.partial(lax.all_gather, axis_name="shard", axis=0, tiled=True)
        return (
            gather(norm1_scale),
            gather(qkv_weight).reshape(width, 3, width).transpose(1, 0, 2),
            gather(out_weight),
            gather(norm2_scale),
            gather(in_weight),
            gather(mlp_out_weight),
        )
    rows = padded_rows(width, hidden)
    reps = lax.axis_size("rep")
    packed = pack(
        norm1_scale[None],
        by_thirds(qkv_weight, 1, width),
        out_weight[None],
        norm2_scale[None],
        by_thirds(in_weight, 1, width),
        mlp_out_weight[None],
        rows,
    )
    packed = lane_chunks(packed.reshape(reps, rows // reps, width))
    everything = join_lanes(gather_call(packed, shards, 0))
    everything = everything.transpose(1, 0, 2, 3).reshape(shards, rows, width)
    norm1, qkv, out, norm2, into, mlp = unpack(everything, n, hidden_n)
    return (
        norm1.reshape(width),
        qkv.reshape(shards, 3, n, width).transpose(1, 0, 2, 3).reshape(3, width, width),
        out.reshape(width, width),
        norm2.reshape(width),
        join_lanes(into.reshape(shards, 3, n, width).transpose(1, 0, 2, 3)).reshape(
            width, 3 * width
        ),
        mlp.reshape(hidden, width),
    )


def reduce_grads(grads):
    g1, gqkv, gout, g2, gin, gmlp = (item.astype(jnp.bfloat16) for item in grads)
    width, hidden = gout.shape[0], gmlp.shape[0]
    shards, reps = lax.axis_size("shard"), lax.axis_size("rep")
    n, hidden_n = width // shards, hidden // shards
    if not can_use_kernels(width, hidden):

        def one(grad):
            part = lax.psum_scatter(grad, "shard", scatter_dimension=0, tiled=True)
            return lax.psum(part, "rep").astype(jnp.float32)

        gqkv = gqkv.transpose(1, 0, 2).reshape(width, 3 * width)
        return tuple(one(item) for item in (g1, gqkv, gout, g2, gin, gmlp))
    rows = padded_rows(width, hidden)
    packed = pack(
        g1.reshape(shards, n),
        gqkv.reshape(3, shards, n, width).transpose(1, 0, 2, 3).reshape(shards, 3 * n, width),
        gout.reshape(shards, n, width),
        g2.reshape(shards, n),
        by_thirds(gin, shards, width),
        gmlp.reshape(shards, hidden_n, width),
        rows,
    )
    packed = packed.reshape(shards, reps, rows // reps, width).transpose(1, 0, 2, 3)
    owned = join_lanes(reduce_call(lane_chunks(packed), 1)).reshape(1, rows, width)
    norm1, qkv, out, norm2, into, mlp = unpack(owned, n, hidden_n)
    wide = [join_lanes(item.reshape(3, n, width)) for item in (qkv, into)]
    return (norm1[0], wide[0], out[0], norm2[0], wide[1], mlp[0])


def per_device(
    hidden_in,
    seq_lengths,
    norm1_scale,
    qkv_weight,
    out_weight,
    norm2_scale,
    in_weight,
    mlp_out_weight,
    cotangent,
):
    token_rows, model_width = hidden_in.shape
    head_width = model_width // HEADS
    cosine, sine, segment, valid_rows = rotary_tables(seq_lengths[0], token_rows, head_width)
    cos_wide = jnp.concatenate([cosine] * 4, axis=1)
    sin_wide = jnp.concatenate([-sine, sine] * 2, axis=1)
    segc, segr = segment[:, None], segment[None, :]
    gain1, w_qkv, w_out, gain2, w_in, w_mlp = gather_weights(
        norm1_scale, qkv_weight, out_weight, norm2_scale, in_weight, mlp_out_weight
    )
    gain1, gain2 = gain1.astype(jnp.float32), gain2.astype(jnp.float32)
    inputs_f32 = hidden_in.astype(jnp.float32)
    normed_one, norm_one_back = jax.vjp(layer_norm, inputs_f32, gain1)
    normed_one = normed_one.astype(jnp.bfloat16)
    qkv, attn_low, lse = attn_forward(normed_one, w_qkv, cos_wide, sin_wide, segc, segr)
    resid_one = inputs_f32 + nn(attn_low, w_out)
    normed_two, norm_two_back = jax.vjp(layer_norm, resid_one, gain2)
    normed_two = normed_two.astype(jnp.bfloat16)
    gate_up = nn(normed_two, w_in)
    mixed, geglu_back = jax.vjp(geglu, gate_up)
    mixed_low = mixed.astype(jnp.bfloat16)
    output = (valid_rows[:, None] * (resid_one + nn(mixed_low, w_mlp))).astype(jnp.bfloat16)

    cot_rows = cotangent.astype(jnp.float32) * valid_rows[:, None]
    mlp_cot = cot_rows.astype(jnp.bfloat16)
    grad_mlp_out = jnp.einsum("nf,nd->fd", mixed_low, mlp_cot, preferred_element_type=jnp.float32)
    grad_mixed = nt(mlp_cot, w_mlp)
    grad_gate_up = geglu_back(grad_mixed)[0].astype(jnp.bfloat16)
    grad_in_w = jnp.einsum(
        "nd,nf->df", normed_two, grad_gate_up, preferred_element_type=jnp.float32
    )
    grad_normed_two = nt(grad_gate_up, w_in)
    grad_resid_ln, grad_gain_two = norm_two_back(grad_normed_two)
    grad_resid = cot_rows + grad_resid_ln
    attn_cot = grad_resid.astype(jnp.bfloat16)
    grad_out_w = jnp.einsum("nd,ne->de", attn_low, attn_cot, preferred_element_type=jnp.float32)
    grad_attn = nt(attn_cot, w_out).astype(jnp.bfloat16)
    grad_qkv = attn_backward(qkv, attn_low, grad_attn, lse, cos_wide, sin_wide, segc, segr)
    grad_qkv_w = jnp.einsum(
        "nd,cne->cde", normed_one, grad_qkv, preferred_element_type=jnp.float32
    )
    grad_normed_one = jnp.einsum(
        "cne,cde->nd", grad_qkv, w_qkv, preferred_element_type=jnp.float32
    )
    grad_input_ln, grad_gain_one = norm_one_back(grad_normed_one)
    input_grad = (grad_resid + grad_input_ln).astype(jnp.bfloat16)
    owned = reduce_grads(
        (grad_gain_one, grad_qkv_w, grad_out_w, grad_gain_two, grad_in_w, grad_mlp_out)
    )
    return (output, input_grad) + owned


def solution(mesh):
    rows = P(("rep", "shard"), None)
    weights = (P("shard"), P("shard", None), P("shard", None), P("shard"), P("shard", None), P("shard", None))
    return jax.shard_map(
        per_device,
        mesh=mesh,
        in_specs=(rows, rows) + weights + (rows,),
        out_specs=(rows, rows) + weights,
        check_vma=False,
    )
```
